256 devices in a mesh: replica: 16 (over z_hi, x), fsdp: 16 (over z_lo, y, core).
Axes of the slice: x: 4, y: 4, z: 8 (z_hi: 4, z_lo: 2; z = z_hi * 2 + z_lo), core: 2. Of those that a mesh axis runs over, the one named last changes fastest.
Arguments:
- inputs: bfloat16 [16, 3072, 8192], P('replica', 'fsdp'), may hold values from -6 to 6
- out_grad: bfloat16 [16, 3072, 8192], P('replica', 'fsdp'), may hold values from -6 to 6
- queries: bfloat16 [16, 3072, 256], P('replica', 'fsdp'), may hold values from -5.5 to 5.5
- key_states: bfloat16 [16, 3072, 128], P('replica', 'fsdp'), may hold values from -5.5 to 5.5
- value_states: bfloat16 [16, 3072, 128], P('replica', 'fsdp'), may hold values from -6 to 6
- weights: bfloat16 [16, 8192, 768], P('replica', 'fsdp'), may hold values from -0.0625 to 0.0625
- frag_delta: float32 [16, 8192, 128], P('replica', 'fsdp'), may hold values from -6 to 6
- frag_params: float32 [8192, 128], P('fsdp'), may hold values from -6 to 6
- frag_moment: float32 [8192, 128], P('fsdp'), may hold values from -3 to 3
Outputs:
- input_grad: bfloat16 [16, 3072, 8192], P('replica', 'fsdp')
- weight_grad: bfloat16 [16, 8192, 768], P('replica', 'fsdp')
- new_params: float32 [8192, 128], P('fsdp')
- new_moment: float32 [8192, 128], P('fsdp')
The draws below stay inside these ranges and needn't reach their ends.
All inputs are finite; a program needn't handle non-finite values.
Results may differ from the reference program's by a relative error of at most 0.027.
Values may be sent and summed in bfloat16 or wider, within the bound.
A program may use at most 128 MiB of HBM per device.

```python
import math
import jax
import jax.numpy as jnp
from jax import lax

D = 8192
HD = 128
HQ = 2
TOK_DEV = 192
SEQUENCE_LENGTH = 3072
WCOLS = 768
N_REPLICA = 16
N_FSDP = 16


def paired_states(key):
    normal_qkey, normal_kkey = jax.random.split(key, 2)
    query_shape = (N_REPLICA, SEQUENCE_LENGTH, HQ * HD)
    key_shape = (N_REPLICA, SEQUENCE_LENGTH, HD)
    normal_q = jnp.clip(jax.random.normal(normal_qkey, query_shape, jnp.float32) * 1.4, -5.5, 5.5)
    gaussian_keys = jnp.clip(jax.random.normal(normal_kkey, key_shape, jnp.float32) * 1.4, -5.5, 5.5)
    query_rows = normal_q
    key_row_block = gaussian_keys
    positions = jnp.arange(SEQUENCE_LENGTH)[None, :, None]
    for marker in range(3):
        target = SEQUENCE_LENGTH - 1 - marker * (SEQUENCE_LENGTH // 4)
        at_target = positions == target
        before = positions == target - 1
        new_keys = jnp.where(at_target, key_row_block, key_row_block)
        new_keys = jnp.where(before, new_keys, new_keys)
        query_rows = jnp.where(at_target, query_rows, query_rows)
        key_row_block = new_keys
    return (query_rows, key_row_block)


def draw_queries(key, part):
    query_rows, key_row_block = paired_states(key)
    return query_rows.astype(jnp.bfloat16)


def draw_key_states(key, part):
    query_rows, key_row_block = paired_states(key)
    return key_row_block.astype(jnp.bfloat16)


def spiked(array, stream_key, source, target, shards_of, factor):
    def block_of(axis_at):
        return (jnp.arange(array.shape[axis_at]) // (array.shape[axis_at] // shards_of)).reshape((-1,) + (1,) * (array.ndim - 1 - axis_at))

    near = jax.random.permutation(stream_key, shards_of)[block_of(target)]
    other_side = (block_of(target) + shards_of // 2) % shards_of
    return jnp.where((block_of(source) == near) | (block_of(source) == other_side), factor * array, array)


def block_levels(rng, shape, shards, least, top_value):
    def one(axis_at, blocks):
        draws = jax.random.uniform(jax.random.fold_in(jax.random.fold_in(rng, 6), axis_at), (blocks,), jnp.float32, least / len(shards), top_value / len(shards))
        return jnp.repeat(jnp.exp(draws), shape[axis_at] // blocks).reshape((-1,) + (1,) * (len(shape) - axis_at - 1))

    level = one(*shards[0])
    for cut in shards[1:]:
        level = level * one(*cut)
    return level


def centred(own_key, dims, spread, bound, cuts=(), kind=jnp.bfloat16):
    loudness = block_levels(own_key, dims, cuts, -0.22, 0.18) if cuts else 1.0
    entries = jax.random.normal(own_key, dims, jnp.float32) * spread * loudness
    return jnp.minimum(jnp.maximum(entries, -bound), bound).astype(kind)


def noise_with(own_key, extent, spread, most, cuts, heavy, kind=jnp.bfloat16):
    entries = spread * jax.random.normal(own_key, extent, jnp.float32)
    if cuts:
        entries = entries * block_levels(own_key, extent, cuts, -0.22, 0.18)
    return jnp.clip(spiked(entries, jax.random.fold_in(own_key, 3), *heavy), -most, most).astype(kind)


def setup_inputs(seed: int = 0) -> dict:
    key_of = jax.random.split(jax.random.key(seed), 10)
    return {
        "inputs": noise_with(key_of[0], (N_REPLICA, SEQUENCE_LENGTH, D), 1.0, 6.0, ((0, 16), (1, 16)), (1, 2, 16, 2.0)),
        "out_grad": noise_with(key_of[1], (N_REPLICA, SEQUENCE_LENGTH, D), 1.0, 6.0, ((0, 16), (1, 16)), (1, 2, 16, 2.0)),
        "queries": draw_queries(jax.random.fold_in(key_of[9], 71), 0),
        "key_states": draw_key_states(jax.random.fold_in(key_of[9], 71), 0),
        "value_states": centred(key_of[4], (N_REPLICA, SEQUENCE_LENGTH, HD), 1.0, 6.0, ((0, 16), (1, 16))),
        "weights": centred(key_of[5], (N_REPLICA, D, WCOLS), D ** -0.5, 0.0625, ((0, 16), (1, 16))),
        "frag_delta": centred(key_of[6], (N_REPLICA, D, HD), 1.0, 6.0, ((0, 16), (1, 16)), jnp.float32),
        "frag_params": centred(key_of[7], (D, HD), 1.0, 6.0, ((0, 16),), jnp.float32),
        "frag_moment": centred(key_of[8], (D, HD), 0.5, 3.0, ((0, 16),), jnp.float32),
    }


rope_base = 500000.0
outer_rate = 0.7
outer_beta = 0.9
masked_score = -1e+30

def rotate_back(gradient, positions):
    head_dim = gradient.shape[-1]
    half_dim = head_dim // 2
    inverse_freq = jnp.exp(-math.log(rope_base) * 2.0 * jnp.arange(half_dim, dtype=jnp.float32) / head_dim)
    angles = positions.astype(jnp.float32)[:, None] * inverse_freq[None, :]
    cosine_part = jnp.cos(angles)[:, None, :]
    sine_part = jnp.sin(angles)[:, None, :]
    low_half = gradient[..., :half_dim]
    high_half = gradient[..., half_dim:]
    return jnp.concatenate([low_half * cosine_part + high_half * sine_part, high_half * cosine_part - low_half * sine_part], axis=-1)

def round_keep(values):
    return lax.optimization_barrier(values.astype(jnp.bfloat16)).astype(jnp.float32)

def one_replica(operands):
    inputs, out_grad, queries, key_states, value_states, weights = operands
    width_qkv = (HQ + 2) * HD
    score_scale = 1.0 / math.sqrt(HD)
    attn_grad = jnp.dot(out_grad, weights[:, width_qkv:], preferred_element_type=jnp.float32).astype(jnp.bfloat16)
    key_float = key_states.astype(jnp.float32)
    value_float = value_states.astype(jnp.float32)
    key_pos = jnp.arange(SEQUENCE_LENGTH, dtype=jnp.int32)

    def attend(running, block_index):
        key_sum, value_sum = running
        offset = block_index * TOK_DEV
        block_q = lax.dynamic_slice_in_dim(queries, offset, TOK_DEV, 0).astype(jnp.float32).reshape(TOK_DEV, HQ, HD)
        block_g = lax.dynamic_slice_in_dim(attn_grad, offset, TOK_DEV, 0).astype(jnp.float32).reshape(TOK_DEV, HQ, HD)
        query_pos = offset + jnp.arange(TOK_DEV, dtype=jnp.int32)
        visible = key_pos[None, :] <= query_pos[:, None]
        scores = jnp.einsum('thd,kd->htk', block_q, key_float) * score_scale
        scores = jnp.where(visible[None], scores, masked_score)
        row_peak = lax.optimization_barrier(jnp.max(scores, axis=-1, keepdims=True))
        exponent = jnp.exp(scores - row_peak)
        attn_probs = exponent / lax.optimization_barrier(jnp.sum(exponent, axis=-1, keepdims=True))
        probs_low = attn_probs.astype(jnp.bfloat16).astype(jnp.float32)
        attended = jnp.einsum('htk,kd->thd', probs_low, value_float).astype(jnp.bfloat16).reshape(TOK_DEV, HQ * HD)
        prob_grad = jnp.einsum('thd,kd->htk', block_g, value_float)
        row_delta = lax.optimization_barrier(jnp.sum(attn_probs * prob_grad, axis=-1, keepdims=True))
        score_grad = (attn_probs * (prob_grad - row_delta) * score_scale).astype(jnp.bfloat16).astype(jnp.float32)
        query_grad = jnp.einsum('htk,kd->thd', score_grad, key_float)
        key_term = jnp.einsum('htk,thd->kd', score_grad, block_q)
        value_term = jnp.einsum('htk,thd->kd', probs_low, block_g)
        return ((key_sum + round_keep(key_term), value_sum + round_keep(value_term)), (attended, query_grad))
    zeros_kv = jnp.zeros((SEQUENCE_LENGTH, HD), jnp.float32)
    (key_sum, value_sum), (attended_all, query_all) = lax.scan(attend, (zeros_kv, zeros_kv), jnp.arange(N_FSDP, dtype=jnp.int32))
    attended_all = attended_all.reshape(SEQUENCE_LENGTH, HQ * HD)
    query_all = query_all.reshape(SEQUENCE_LENGTH, HQ, HD)
    query_grad = rotate_back(query_all, key_pos).astype(jnp.bfloat16).reshape(SEQUENCE_LENGTH, HQ * HD)
    key_grad = rotate_back(key_sum[:, None, :], key_pos)[:, 0, :].astype(jnp.bfloat16)
    value_grad = value_sum.astype(jnp.bfloat16)
    proj_grad = jnp.concatenate([query_grad, key_grad, value_grad], axis=1)
    input_grad = jnp.dot(proj_grad, weights[:, :width_qkv].T, preferred_element_type=jnp.float32).astype(jnp.bfloat16)

    def accumulate(running, block_index):
        offset = block_index * TOK_DEV
        act_block = lax.dynamic_slice_in_dim(inputs, offset, TOK_DEV, 0)
        grad_block = lax.dynamic_slice_in_dim(out_grad, offset, TOK_DEV, 0)
        proj_block = lax.dynamic_slice_in_dim(proj_grad, offset, TOK_DEV, 0)
        attn_block = lax.dynamic_slice_in_dim(attended_all, offset, TOK_DEV, 0)
        qkv_term = jnp.dot(act_block.T, proj_block, preferred_element_type=jnp.float32)
        out_term = jnp.dot(grad_block.T, attn_block, preferred_element_type=jnp.float32)
        return (running + round_keep(jnp.concatenate([qkv_term, out_term], axis=1)), None)
    weight_sum, unused = lax.scan(accumulate, jnp.zeros((D, WCOLS), jnp.float32), jnp.arange(N_FSDP, dtype=jnp.int32))
    return (input_grad, weight_sum.astype(jnp.bfloat16))

def reference(inputs, out_grad, queries, key_states, value_states, weights, frag_delta, frag_params, frag_moment):
    input_grad, weight_grad = lax.map(one_replica, (inputs, out_grad, queries, key_states, value_states, weights))
    outer_grad = lax.optimization_barrier(jnp.sum(frag_delta, axis=0)) / N_REPLICA
    new_moment = outer_beta * frag_moment + outer_grad
    new_params = frag_params - outer_rate * (outer_grad + outer_beta * new_moment)
    return (input_grad, weight_grad, new_params, new_moment)
```

```python
import functools
import math

import jax
import jax.numpy as jnp
from jax import lax
from jax.experimental import pallas as pl
from jax.experimental.pallas import tpu as pltpu
from jax.sharding import PartitionSpec as P

rope_base = 500000.0
outer_rate = 0.7
outer_beta = 0.9
masked_score = -1e30

BF = jnp.bfloat16
F32 = jnp.float32
MESH = pl.DeviceIdType.MESH

TOK = 192
PAIR = 2 * TOK
HD = 128
QW = 256
BLK = 512
WC = 768
QKV = 512
CHIPS = 8
YS = 4

GA = 288
SA = 144
SA1 = 64
SB1 = 208
PART = 256

NT = (((1,), (1,)), ((), ()))
TN = (((0,), (0,)), ((), ()))


def dot(a, b):
    return jnp.dot(a, b, preferred_element_type=F32)


def dot_nt(a, b):
    return lax.dot_general(a, b, NT, preferred_element_type=F32)


def dot_tn(a, b):
    return lax.dot_general(a, b, TN, preferred_element_type=F32)


def kernel(
    replicas,
    inputs,
    out_grad,
    queries,
    keys,
    values,
    weights,
    delta,
    params,
    moment,
    cosines,
    sines,
    input_out,
    weight_out,
    params_out,
    moment_out,
    xi,
    xg,
    wg,
    kb,
    vb,
    qs,
    st,
    plow,
    row_sum,
    att_t,
    dq_t,
    gs,
    agp,
    agr,
    att,
    proj,
    dkv,
    sk,
    ps,
    rk,
    dw,
    rz,
    ra1,
    ra2,
    rb1,
    rb2,
    rf,
    rg,
    rw,
    ig,
    wout,
    cs,
    sn,
    fd,
    fb,
    fr,
    fz,
    fzr,
    fs,
    fp,
    fm,
    lsem,
    ssem,
    rsem,
    bsem,
    brsem,
):
    r = lax.axis_index("replica")
    f = lax.axis_index("fsdp")
    c = lax.rem(f, 2)
    y = lax.rem(f // 2, YS)
    z = f // (2 * YS)
    o = 1 - c
    x = lax.rem(r, 4)
    zh = r // 4

    def chip(dz, dy):
        return lax.rem(z + dz, 2) * YS + lax.rem(y + dy, YS)

    def at(dz, dy, core=None):
        return (r, chip(dz, dy) * 2 + (c if core is None else core))

    yp, ym, zp, sib = at(0, 1), at(0, 3), at(1, 0), at(0, 0, o)

    def back(s):
        return (s // 4) * 4 + (4 - s % 4) % 4

    made = []

    def remote(src, dst, dev):
        i = len(made)
        copy = pltpu.make_async_remote_copy(
            src_ref=src,
            dst_ref=dst,
            send_sem=ssem.at[i],
            recv_sem=rsem.at[i],
            device_id=dev,
            device_id_type=MESH,
        )
        made.append(copy)
        return copy

    local_made = []

    def local(src, dst):
        copy = pltpu.make_async_copy(src, dst, lsem.at[len(local_made)])
        local_made.append(copy)
        copy.start()
        return copy

    def slot_chip(s):
        return lax.rem(z + s // 4, 2) * YS + lax.rem(y + s % 4, YS)

    def columns(s, core):
        return pl.ds(pl.multiple_of((slot_chip(s) * 2 + core) * BLK, BLK), BLK)

    load_q = [local(queries.at[0, :, pl.ds(h * HD, HD)], qs.at[pl.ds(h * TOK, TOK)]) for h in (0, 1)]
    load_k = local(keys.at[0], kb.at[0, c])
    load_v = local(values.at[0], vb.at[0, c])
    load_w = local(weights.at[0], wg.at[0])
    load_d = local(delta.at[0], fd)
    load_g = [local(out_grad.at[0, :, columns(s, c)], xg.at[s, c]) for s in range(CHIPS)]
    load_x = [local(inputs.at[0, :, columns(s, c)], xi.at[s, c]) for s in range(CHIPS)]
    load_t = [local(cosines, cs), local(sines, sn), local(params, fp), local(moment, fm)]

    peers = [at(s // 4, s % 4) for s in range(1, CHIPS)] + [sib]
    x_peers = [(zh * 4 + lax.rem(x + d, 4), f) for d in (1, 2, 3)]
    z_peers = [(lax.rem(zh + d, 4) * 4 + x, f) for d in (1, 2, 3)]
    barrier = pltpu.get_barrier_semaphore()
    for dev in peers + x_peers + z_peers:
        pl.semaphore_signal(barrier, inc=1, device_id=dev, device_id_type=MESH)
    pl.semaphore_wait(barrier, len(peers) + 6)

    order = (1, 3, 4, 5, 7, 2, 6)
    send_k = {back(s): remote(keys.at[0], kb.at[back(s), c], at(s // 4, s % 4)) for s in order}
    send_v = {back(s): remote(values.at[0], vb.at[back(s), c], at(s // 4, s % 4)) for s in order}
    for copy in send_k.values():
        copy.start()
    for copy in send_v.values():
        copy.start()
    cross_k = [remote(keys.at[0], kb.at[0, c], sib)]
    cross_v = [remote(values.at[0], vb.at[0, c], sib)]
    cross_k[0].start()
    cross_v[0].start()

    class Gather:
        def __init__(self, first, width):
            cols = pl.ds(first, width)
            own = weights.at[0, :, cols]

            def rows(s, lo, hi):
                return wg.at[s, pl.ds(lo, hi - lo), cols]

            def move(src, dst, lo, hi, dev):
                return remote(rows(src, lo, hi), rows(dst, lo, hi), dev)

            self.s3 = remote(own, wg.at[3, :, cols], yp)
            self.s1 = remote(own, wg.at[1, :, cols], ym)
            self.s4 = remote(own, wg.at[4, :, cols], zp)
            half = GA // 2
            self.s2a = move(1, 2, 0, BLK // 2, ym)
            self.s2b = move(3, 2, BLK // 2, BLK, yp)
            self.s5b = move(1, 5, GA, BLK, zp)
            self.s7b = move(3, 7, GA, BLK, zp)
            self.s7a = move(4, 7, 0, GA, yp)
            self.s5a = move(4, 5, 0, GA, ym)
            self.s6b = move(2, 6, GA, BLK, zp)
            self.s6a1 = move(5, 6, 0, half, ym)
            self.s6a2 = move(7, 6, half, GA, yp)

        def wave0(self):
            self.s3.start()
            self.s1.start()
            self.s4.start()

        def wave1(self):
            self.s1.wait_recv()
            self.s2a.start()
            self.s5b.start()
            self.s3.wait_recv()
            self.s2b.start()
            self.s7b.start()
            self.s4.wait_recv()
            self.s7a.start()
            self.s5a.start()

        def wave2(self):
            self.s2a.wait_recv()
            self.s2b.wait_recv()
            self.s6b.start()
            self.s5a.wait_recv()
            self.s6a1.start()
            self.s7a.wait_recv()
            self.s6a2.start()

        def finish(self):
            for copy in (self.s5b, self.s7b, self.s6b, self.s6a1, self.s6a2):
                copy.wait_recv()

    gather_o = Gather(QKV, QW)
    gather_q = Gather(0, QW)
    gather_k = Gather(QW, QW)
    gather_o.wave0()

    cross_g = [remote(out_grad.at[0, :, columns(s, o)], xg.at[s, c], sib) for s in range(CHIPS)]
    cross_x = [remote(inputs.at[0, :, columns(s, o)], xi.at[s, c], sib) for s in range(CHIPS)]
    for copy in cross_g:
        copy.start()

    load_d.wait()
    for j in range(4):
        fb[j] = fd[pl.ds(j * 128, 128), :].astype(BF)
    frag_x = [remote(fb.at[lax.rem(x + d, 4)], fr.at[d - 1], x_peers[d - 1]) for d in (1, 2, 3)]
    for copy in frag_x:
        copy.start()

    for copy in load_q:
        copy.wait()
    load_k.wait()
    load_v.wait()
    load_w.wait()
    for s in order:
        send_k[s].wait_recv()
        cross_k.append(remote(kb.at[s, c], kb.at[s, c], sib))
        cross_k[-1].start()
    for copy in cross_k:
        copy.wait_recv()

    scale = 1.0 / math.sqrt(HD)

    def score_step(s, peak):
        part = dot_nt(kb[s].reshape(PAIR, HD), qs[...]) * scale
        key_pos = slot_chip(s) * PAIR + lax.broadcasted_iota(jnp.int32, (PAIR, PAIR), 0)
        lane = lax.broadcasted_iota(jnp.int32, (1, PAIR), 1)
        query_pos = f * TOK + jnp.where(lane >= TOK, lane - TOK, lane)
        part = jnp.where(key_pos <= query_pos, part, masked_score)
        st[s] = part
        return jnp.maximum(peak, jnp.max(part, axis=0, keepdims=True))

    peak = lax.fori_loop(0, CHIPS, score_step, jnp.full((1, PAIR), masked_score, F32))

    def exp_step(s, total):
        part = jnp.exp(st[s] - peak)
        st[s] = part
        return total + jnp.sum(part, axis=0, keepdims=True)

    total = lax.fori_loop(0, CHIPS, exp_step, jnp.zeros((1, PAIR), F32))
    inverse = 1.0 / total

    for s in order:
        send_v[s].wait_recv()
        cross_v.append(remote(vb.at[s, c], vb.at[s, c], sib))
        cross_v[-1].start()
    for copy in cross_v:
        copy.wait_recv()

    att_t[...] = jnp.zeros_like(att_t)

    def value_step(s, carry):
        part = st[s] * inverse
        st[s] = part
        low = part.astype(BF)
        plow[s] = low
        att_t[...] += dot_tn(vb[s].reshape(PAIR, HD), low)
        return carry

    lax.fori_loop(0, CHIPS, value_step, 0)

    attended = att_t[...].T.astype(BF)
    for h in (0, 1):
        att[c, :, pl.ds(h * HD, HD)] = attended[h * TOK : (h + 1) * TOK]
    cross_a = remote(att.at[c], att.at[c], sib)
    cross_a.start()

    for copy in frag_x:
        copy.wait_recv()
    partial = fd[pl.ds(pl.multiple_of(x * 128, 128), 128), :]
    for d in range(3):
        partial = partial + fr[d].astype(F32)
    fs[...] = partial
    fz[...] = partial.astype(BF).reshape(4, 32, 128)
    frag_z = [remote(fz.at[lax.rem(zh + d, 4)], fzr.at[d - 1], z_peers[d - 1]) for d in (1, 2, 3)]
    for copy in frag_z:
        copy.start()

    gather_o.wave1()
    gather_o.wave2()
    gather_q.wave0()
    for copy in cross_x:
        copy.start()

    for copy in load_g:
        copy.wait()
    for copy in cross_g:
        copy.wait_recv()
    gather_o.finish()
    agp[...] = jnp.zeros_like(agp)

    def grad_step(s, carry):
        part = dot(xg[s].reshape(PAIR, BLK), wg[s, :, pl.ds(QKV, QW)])
        agp[...] += part.reshape(2, TOK, QW)
        return carry

    lax.fori_loop(0, CHIPS, grad_step, 0)
    cross_p = remote(agp.at[o], agr, sib)
    cross_p.start()
    cross_p.wait_recv()
    grad = (agp[c] + agr[...]).astype(BF)
    for h in (0, 1):
        gs[pl.ds(h * TOK, TOK), :] = grad[:, h * HD : (h + 1) * HD]
    row_delta = jnp.sum(att_t[...] * gs[...].astype(F32).T, axis=0, keepdims=True)

    gather_q.wave1()

    dq_t[...] = jnp.zeros_like(dq_t)

    def cross_copy(s):
        return pltpu.make_async_remote_copy(
            src_ref=dkv.at[s, o],
            dst_ref=sk.at[s],
            send_sem=bsem.at[s],
            recv_sem=brsem.at[s],
            device_id=sib,
            device_id_type=MESH,
        )

    def back_step(s, carry):
        prob_grad = dot_nt(vb[s].reshape(PAIR, HD), gs[...])
        low = (st[s] * (prob_grad - row_delta) * scale).astype(BF)
        dq_t[...] += dot_tn(kb[s].reshape(PAIR, HD), low)
        dkv[s, :, :, pl.ds(0, HD)] = dot(low, qs[...]).astype(BF).reshape(2, TOK, HD)
        dkv[s, :, :, pl.ds(HD, HD)] = dot(plow[s], gs[...]).astype(BF).reshape(2, TOK, HD)
        cross_copy(s).start()
        return carry

    lax.fori_loop(0, CHIPS, back_step, 0)

    def pair_step(s, carry):
        cross_copy(s).wait_recv()
        ps[s] = (dkv[s, c].astype(F32) + sk[s].astype(F32)).astype(BF)
        return carry

    lax.fori_loop(0, CHIPS, pair_step, 0)
    send_d = {back(s): remote(ps.at[s], rk.at[back(s)], at(s // 4, s % 4)) for s in order}
    for copy in send_d.values():
        copy.start()
    gather_q.wave2()
    gather_k.wave0()

    for copy in load_t:
        copy.wait()

    def rotate(values_in):
        return values_in * cs[...] + pltpu.roll(values_in, HD // 2, 1) * sn[...]

    dq = dq_t[...].T
    for h in (0, 1):
        proj[c, :, pl.ds(h * HD, HD)] = rotate(dq[h * TOK : (h + 1) * TOK]).astype(BF)
    cross_q = remote(proj.at[c, :, pl.ds(0, QW)], proj.at[c, :, pl.ds(0, QW)], sib)
    cross_q.start()

    class Scatter:
        def __init__(self, p):
            self.p = p
            part = dw.at[p]
            self.to_z = remote(part.at[pl.ds(4, 4), pl.ds(SA, PART - SA)], rz.at[p], zp)
            self.a_up = [remote(part.at[s, pl.ds(0, SA1)], ra1.at[p, i], yp) for i, s in enumerate((2, 6))]
            self.a_down = [
                remote(part.at[s, pl.ds(SA1, SA - SA1)], ra2.at[p, i], ym) for i, s in enumerate((2, 6))
            ]
            self.b_up = remote(part.at[2, pl.ds(SA, SB1 - SA)], rb1.at[p], yp)
            self.b_down = remote(part.at[2, pl.ds(SB1, PART - SB1)], rb2.at[p], ym)
            self.f_up = remote(part.at[1], rf.at[p, 0], yp)
            self.g_up = remote(part.at[5, pl.ds(0, SA)], rg.at[p, 0], yp)
            self.f_down = remote(part.at[3], rf.at[p, 1], ym)
            self.g_down = remote(part.at[7, pl.ds(0, SA)], rg.at[p, 1], ym)
            self.last = remote(part.at[4, pl.ds(0, SA)], rw.at[p], zp)

        def add(self, s, lo, hi, *others):
            rows = pl.ds(lo, hi - lo)
            value = dw[self.p, s, rows, :].astype(F32)
            for other in others:
                value = value + other[...].astype(F32)
            dw[self.p, s, rows, :] = value.astype(BF)

        def step1(self):
            self.to_z.start()
            for copy in self.a_up + self.a_down:
                copy.start()

        def step2(self):
            self.to_z.wait_recv()
            self.add(2, SA, PART, rz.at[self.p, 2])
            self.b_up.start()
            self.b_down.start()
            for s in (1, 3, 0):
                self.add(s, SA, PART, rz.at[self.p, s])

        def step3(self):
            p = self.p
            for copy in self.a_up + [self.b_up]:
                copy.wait_recv()
            self.add(5, 0, SA1, ra1.at[p, 1])
            self.g_up.start()
            self.add(1, 0, SA1, ra1.at[p, 0])
            self.add(1, SA, SB1, rb1.at[p])
            self.f_up.start()
            for copy in self.a_down + [self.b_down]:
                copy.wait_recv()
            self.add(7, SA1, SA, ra2.at[p, 1])
            self.g_down.start()
            self.add(3, SA1, SA, ra2.at[p, 0])
            self.add(3, SB1, PART, rb2.at[p])
            self.f_down.start()

        def step4(self):
            self.g_up.wait_recv()
            self.g_down.wait_recv()
            self.add(4, 0, SA, rg.at[self.p, 0], rg.at[self.p, 1])
            self.last.start()

        def step5(self, first):
            p = self.p
            self.f_up.wait_recv()
            self.f_down.wait_recv()
            self.last.wait_recv()
            value = dw[p, 0].astype(F32) + rf[p, 0].astype(F32) + rf[p, 1].astype(F32)
            top = value[:SA] + rw[p].astype(F32)
            value = jnp.concatenate([top, value[SA:]], axis=0)
            wout[:, pl.ds(first, PART)] = value.T.astype(BF)

    scatter_o, scatter_q, scatter_k = Scatter(0), Scatter(1), Scatter(2)

    def outer(p, left, right):
        def step(s, carry):
            dw[p, s] = dot(left, right[s].reshape(PAIR, BLK)).astype(BF)
            return carry

        lax.fori_loop(0, CHIPS, step, 0)

    cross_a.wait_recv()
    outer(0, att[...].reshape(PAIR, QW).T, xg)

    for copy in frag_z:
        copy.wait_recv()
    own = fs[pl.ds(pl.multiple_of(zh * 32, 32), 32), :]
    for d in range(3):
        own = own + fzr[d].astype(F32)
    fs[pl.ds(pl.multiple_of(zh * 32, 32), 32), :] = own
    home_z = pl.ds(pl.multiple_of(zh * 32, 32), 32)
    frag_bz = [remote(fs.at[home_z], fs.at[home_z], dev) for dev in z_peers]
    for copy in frag_z:
        copy.wait_send()
    for copy in frag_bz:
        copy.start()

    gather_k.wave1()
    scatter_o.step1()

    for copy in load_x:
        copy.wait()
    for copy in cross_x:
        copy.wait_recv()
    cross_q.wait_recv()
    outer(1, proj[:, :, pl.ds(0, QW)].reshape(PAIR, QW).T, xi)
    gather_k.wave2()
    scatter_q.step1()

    for copy in send_d.values():
        copy.wait_recv()

    def sum_step(s, carry):
        return carry + rk[s].astype(F32)

    kv = lax.fori_loop(1, CHIPS, sum_step, ps[0].astype(F32))
    proj[c, :, pl.ds(QW, HD)] = rotate(kv[:, :HD]).astype(BF)
    proj[c, :, pl.ds(QW + HD, HD)] = kv[:, HD:].astype(BF)
    cross_kv = remote(proj.at[c, :, pl.ds(QW, QW)], proj.at[c, :, pl.ds(QW, QW)], sib)
    cross_kv.start()
    cross_kv.wait_recv()
    outer(2, proj[:, :, pl.ds(QW, QW)].reshape(PAIR, QW).T, xi)
    scatter_k.step1()

    for copy in frag_bz:
        copy.wait_recv()
    home_x = pl.ds(pl.multiple_of(x * 128, 128), 128)
    for copy in frag_bz:
        copy.wait_send()
    fd[home_x, :] = fs[...]
    frag_bx = [remote(fs, fd.at[home_x], dev) for dev in x_peers]
    for copy in frag_bx:
        copy.start()

    scatter_o.step2()
    gather_q.finish()
    gather_k.finish()

    for s in range(CHIPS):
        ig[s] = dot_nt(proj[...].reshape(PAIR, QKV), wg[s, :, pl.ds(0, QKV)]).astype(BF).reshape(2, TOK, BLK)
        local(ig.at[s, c], input_out.at[0, :, columns(s, c)])
    grad_stores = local_made[-CHIPS:]
    cross_i = [
        remote(ig.at[s, o], input_out.at[0, :, columns(s, c)], sib) for s in range(CHIPS)
    ]
    for copy in cross_i:
        copy.start()

    scatter_o.step3()
    scatter_q.step2()
    scatter_o.step4()
    scatter_q.step3()
    scatter_k.step2()
    scatter_o.step5(QKV)
    scatter_q.step4()
    scatter_k.step3()
    scatter_q.step5(0)
    scatter_k.step4()

    for copy in frag_bx:
        copy.wait_recv()
    outer_grad = fd[...] / replicas
    moment_next = outer_beta * fm[...] + outer_grad
    fm[...] = moment_next
    fp[...] = fp[...] - outer_rate * (outer_grad + outer_beta * moment_next)
    stores = [local(fm, moment_out), local(fp, params_out)]

    scatter_k.step5(QW)
    stores.append(local(wout, weight_out.at[0]))

    for copy in cross_i:
        copy.wait_recv()
    for copy in grad_stores + stores:
        copy.wait()
    waited = frag_z + frag_bz
    for copy in made:
        if not any(copy is other for other in waited):
            copy.wait_send()

    def drain(s, carry):
        cross_copy(s).wait_send()
        return carry

    lax.fori_loop(0, CHIPS, drain, 0)


def body(inputs, out_grad, queries, key_states, value_states, weights, frag_delta, frag_params, frag_moment):
    half = HD // 2
    inverse_freq = jnp.exp(-math.log(rope_base) * 2.0 * jnp.arange(half, dtype=F32) / HD)
    positions = lax.axis_index("fsdp") * TOK + jnp.arange(TOK, dtype=jnp.int32)
    angles = positions.astype(F32)[:, None] * inverse_freq[None, :]
    cosine, sine = jnp.cos(angles), jnp.sin(angles)
    cosines = jnp.concatenate([cosine, cosine], axis=1)
    sines = jnp.concatenate([sine, -sine], axis=1)
    anywhere = pl.BlockSpec(memory_space=pl.ANY)
    vm = pltpu.VMEM
    dma = pltpu.SemaphoreType.DMA
    return pl.pallas_call(
        functools.partial(kernel, float(lax.axis_size("replica"))),
        out_shape=(
            jax.ShapeDtypeStruct(inputs.shape, BF),
            jax.ShapeDtypeStruct(weights.shape, BF),
            jax.ShapeDtypeStruct(frag_params.shape, F32),
            jax.ShapeDtypeStruct(frag_moment.shape, F32),
        ),
        in_specs=[anywhere] * 11,
        out_specs=(anywhere,) * 4,
        scratch_shapes=[
            vm((CHIPS, 2, TOK, BLK), BF),
            vm((CHIPS, 2, TOK, BLK), BF),
            vm((CHIPS, BLK, WC), BF),
            vm((CHIPS, 2, TOK, HD), BF),
            vm((CHIPS, 2, TOK, HD), BF),
            vm((PAIR, HD), BF),
            vm((CHIPS, PAIR, PAIR), F32),
            vm((CHIPS, PAIR, PAIR), BF),
            vm((1, PAIR), F32),
            vm((HD, PAIR), F32),
            vm((HD, PAIR), F32),
            vm((PAIR, HD), BF),
            vm((2, TOK, QW), F32),
            vm((TOK, QW), F32),
            vm((2, TOK, QW), BF),
            vm((2, TOK, QKV), BF),
            vm((CHIPS, 2, TOK, QW), BF),
            vm((CHIPS, TOK, QW), BF),
            vm((CHIPS, TOK, QW), BF),
            vm((CHIPS, TOK, QW), BF),
            vm((3, CHIPS, PART, BLK), BF),
            vm((3, YS, PART - SA, BLK), BF),
            vm((3, 2, SA1, BLK), BF),
            vm((3, 2, SA - SA1, BLK), BF),
            vm((3, SB1 - SA, BLK), BF),
            vm((3, PART - SB1, BLK), BF),
            vm((3, 2, PART, BLK), BF),
            vm((3, 2, SA, BLK), BF),
            vm((3, SA, BLK), BF),
            vm((CHIPS, 2, TOK, BLK), BF),
            vm((BLK, WC), BF),
            vm((TOK, HD), F32),
            vm((TOK, HD), F32),
            vm((512, 128), F32),
            vm((4, 128, 128), BF),
            vm((3, 128, 128), BF),
            vm((4, 32, 128), BF),
            vm((3, 32, 128), BF),
            vm((128, 128), F32),
            vm((512, 128), F32),
            vm((512, 128), F32),
            dma((64,)),
            dma((192,)),
            dma((192,)),
            dma((CHIPS,)),
            dma((CHIPS,)),
        ],
        compiler_params=pltpu.CompilerParams(
            collective_id=0, has_side_effects=True, vmem_limit_bytes=60 * 2**20
        ),
    )(inputs, out_grad, queries, key_states, value_states, weights, frag_delta, frag_params, frag_moment, cosines, sines)


def solution(mesh):
    rows = P("replica", "fsdp", None)
    shared = P("fsdp", None)
    return jax.shard_map(
        body,
        mesh=mesh,
        in_specs=(rows,) * 7 + (shared,) * 2,
        out_specs=(rows, rows, shared, shared),
        check_vma=False,
    )
```

```python
import functools
import math

import jax
import jax.numpy as jnp
from jax import lax
from jax.experimental import pallas as pl
from jax.experimental.pallas import tpu as pltpu
from jax.sharding import PartitionSpec as P

rope_base = 500000.0
outer_rate = 0.7
outer_beta = 0.9
masked_score = -1e30

BF = jnp.bfloat16
F32 = jnp.float32
MESH = pl.DeviceIdType.MESH

TOK = 192
PAIR = 2 * TOK
HD = 128
QW = 256
BLK = 512
WC = 768
QKV = 512
CHIPS = 8
YS = 4

WEIGHT_Z = 288
KEY_Z = 112
GRAD_Z = (160, 128, 128)
MOST_A, MOST_B = 160, 128
PART = 256

NT = (((1,), (1,)), ((), ()))
TN = (((0,), (0,)), ((), ()))


def dot(a, b):
    return jnp.dot(a, b, preferred_element_type=F32)


def dot_nt(a, b):
    return lax.dot_general(a, b, NT, preferred_element_type=F32)


def dot_tn(a, b):
    return lax.dot_general(a, b, TN, preferred_element_type=F32)


def kernel(
    replicas,
    inputs,
    out_grad,
    queries,
    keys,
    values,
    weights,
    delta,
    params,
    moment,
    input_out,
    weight_out,
    params_out,
    moment_out,
    xi,
    xg,
    wg,
    kb,
    vb,
    qs,
    st,
    plow,
    att_t,
    dq_t,
    gs,
    agp,
    agr,
    att,
    proj,
    dkv,
    sk,
    ps,
    rk,
    dw,
    rz,
    ra1,
    ra2,
    rb1,
    rb2,
    rf,
    rg,
    rw,
    ig,
    cs,
    sn,
    fd,
    fb,
    fr,
    fz,
    fzr,
    fs,
    fp,
    fm,
    lsem,
    ssem,
    rsem,
    bsem,
    brsem,
):
    r = lax.axis_index("replica")
    f = lax.axis_index("fsdp")
    c = lax.rem(f, 2)
    y = lax.rem(f // 2, YS)
    z = f // (2 * YS)
    o = 1 - c
    x = lax.rem(r, 4)
    zh = r // 4

    def chip(dz, dy):
        return lax.rem(z + dz, 2) * YS + lax.rem(y + dy, YS)

    def at(dz, dy, core=None):
        return (r, chip(dz, dy) * 2 + (c if core is None else core))

    yp, ym, zp, sib = at(0, 1), at(0, 3), at(1, 0), at(0, 0, o)

    def back(s):
        return (s // 4) * 4 + (4 - s % 4) % 4

    made = []

    def remote(src, dst, dev):
        i = len(made)
        copy = pltpu.make_async_remote_copy(
            src_ref=src,
            dst_ref=dst,
            send_sem=ssem.at[i],
            recv_sem=rsem.at[i],
            device_id=dev,
            device_id_type=MESH,
        )
        made.append(copy)
        return copy

    local_made = []

    def local(src, dst):
        copy = pltpu.make_async_copy(src, dst, lsem.at[len(local_made)])
        local_made.append(copy)
        copy.start()
        return copy

    def slot_chip(s):
        return lax.rem(z + s // 4, 2) * YS + lax.rem(y + s % 4, YS)

    def columns(s, core):
        return pl.ds(pl.multiple_of((slot_chip(s) * 2 + core) * BLK, BLK), BLK)

    load_q = [local(queries.at[0, :, pl.ds(h * HD, HD)], qs.at[pl.ds(h * TOK, TOK)]) for h in (0, 1)]
    load_k = local(keys.at[0], kb.at[0, c])
    load_v = local(values.at[0], vb.at[0, c])
    load_w = local(weights.at[0], wg.at[0])
    load_d = local(delta.at[0], fd)
    load_g = [local(out_grad.at[0, :, columns(s, c)], xg.at[s, c]) for s in range(CHIPS)]
    load_x = [local(inputs.at[0, :, columns(s, c)], xi.at[s, c]) for s in range(CHIPS)]
    load_t = [local(params, fp), local(moment, fm)]

    peers = [at(s // 4, s % 4) for s in range(1, CHIPS)] + [sib]
    x_peers = [(zh * 4 + lax.rem(x + d, 4), f) for d in (1, 2, 3)]
    z_peers = [(lax.rem(zh + d, 4) * 4 + x, f) for d in (1, 2, 3)]
    barrier = pltpu.get_barrier_semaphore()
    for dev in peers + x_peers + z_peers:
        pl.semaphore_signal(barrier, inc=1, device_id=dev, device_id_type=MESH)
    pl.semaphore_wait(barrier, len(peers) + 6)

    class Gather:
        def __init__(self, own, rows, extent, first):
            def move(src, dst, lo, hi, dev):
                return remote(rows(src, lo, hi), rows(dst, lo, hi), dev)

            half = first // 2
            self.s3 = remote(own, rows(3, 0, extent), yp)
            self.s1 = remote(own, rows(1, 0, extent), ym)
            self.s4 = remote(own, rows(4, 0, extent), zp)
            self.s2a = move(1, 2, 0, extent // 2, ym)
            self.s2b = move(3, 2, extent // 2, extent, yp)
            self.s5b = move(1, 5, first, extent, zp)
            self.s7b = move(3, 7, first, extent, zp)
            self.s7a = move(4, 7, 0, first, yp)
            self.s5a = move(4, 5, 0, first, ym)
            self.s6b = move(2, 6, first, extent, zp)
            self.s6a1 = move(5, 6, 0, half, ym)
            self.s6a2 = move(7, 6, half, first, yp)

        def wave0(self):
            self.s3.start()
            self.s1.start()
            self.s4.start()

        def wave1(self):
            self.s1.wait_recv()
            self.s2a.start()
            self.s5b.start()
            self.s3.wait_recv()
            self.s2b.start()
            self.s7b.start()
            self.s4.wait_recv()
            self.s7a.start()
            self.s5a.start()

        def wave2(self):
            self.s2a.wait_recv()
            self.s2b.wait_recv()
            self.s6b.start()
            self.s5a.wait_recv()
            self.s6a1.start()
            self.s7a.wait_recv()
            self.s6a2.start()

        def finish(self):
            for copy in (self.s5b, self.s7b, self.s6b, self.s6a1, self.s6a2):
                copy.wait_recv()

    def gather_states(source, target):
        return Gather(source.at[0], lambda s, lo, hi: target.at[s, c, pl.ds(lo, hi - lo)], TOK, KEY_Z)

    def gather_weights(first):
        cols = pl.ds(first, HD)
        return Gather(
            weights.at[0, :, cols], lambda s, lo, hi: wg.at[s, pl.ds(lo, hi - lo), cols], BLK, WEIGHT_Z
        )

    order = (1, 3, 4, 5, 7, 2, 6)
    gather_key = gather_states(keys, kb)
    gather_value = gather_states(values, vb)
    gather_o = [gather_weights(QKV + HD * i) for i in range(2)]
    gather_q = [gather_weights(HD * i) for i in range(4)]
    gather_key.wave0()
    gather_value.wave0()
    gather_o[0].wave0()
    gather_o[1].wave0()
    cross_k = [remote(keys.at[0] if s == 0 else kb.at[s, c], kb.at[s, c], sib) for s in range(CHIPS)]
    cross_v = [remote(values.at[0] if s == 0 else vb.at[s, c], vb.at[s, c], sib) for s in range(CHIPS)]

    cross_g = [remote(out_grad.at[0, :, columns(s, o)], xg.at[s, c], sib) for s in range(CHIPS)]
    cross_x = [remote(inputs.at[0, :, columns(s, o)], xi.at[s, c], sib) for s in range(CHIPS)]
    for copy in cross_g:
        copy.start()

    load_d.wait()
    for j in range(4):
        fb[j] = fd[pl.ds(j * 128, 128), :].astype(BF)
    frag_x = [remote(fb.at[lax.rem(x + d, 4)], fr.at[d - 1], x_peers[d - 1]) for d in (1, 2, 3)]
    for copy in frag_x:
        copy.start()

    pos = (f * TOK + lax.broadcasted_iota(jnp.int32, (TOK, HD), 0)).astype(F32)
    lane = lax.broadcasted_iota(jnp.int32, (1, HD), 1)
    step_of = jnp.where(lane >= HD // 2, lane - HD // 2, lane).astype(F32)
    angles = pos * jnp.exp(-math.log(rope_base) * 2.0 * step_of / HD)
    cs[...] = jnp.cos(angles)
    sine = jnp.sin(angles)
    sn[...] = jnp.where(lane >= HD // 2, -sine, sine)

    for copy in load_q:
        copy.wait()
    load_k.wait()
    load_v.wait()
    load_w.wait()
    gather_key.wave1()
    gather_value.wave1()
    gather_o[0].wave1()
    gather_o[1].wave1()
    gather_key.wave2()
    gather_value.wave2()
    gather_q[0].wave0()
    gather_o[0].wave2()
    gather_q[1].wave0()
    gather_o[1].wave2()
    gather_key.finish()
    for copy in cross_k:
        copy.start()
    gather_value.finish()
    for copy in cross_v:
        copy.start()
    for copy in cross_x:
        copy.start()
    for copy in cross_k:
        copy.wait_recv()

    scale = 1.0 / math.sqrt(HD)

    def score_step(s, peak):
        part = dot_nt(kb[s].reshape(PAIR, HD), qs[...]) * scale
        key_pos = slot_chip(s) * PAIR + lax.broadcasted_iota(jnp.int32, (PAIR, PAIR), 0)
        lane = lax.broadcasted_iota(jnp.int32, (1, PAIR), 1)
        query_pos = f * TOK + jnp.where(lane >= TOK, lane - TOK, lane)
        part = jnp.where(key_pos <= query_pos, part, masked_score)
        st[s] = part
        return jnp.maximum(peak, jnp.max(part, axis=0, keepdims=True))

    peak = lax.fori_loop(0, CHIPS, score_step, jnp.full((1, PAIR), masked_score, F32))

    def exp_step(s, total):
        part = jnp.exp(st[s] - peak)
        st[s] = part
        return total + jnp.sum(part, axis=0, keepdims=True)

    total = lax.fori_loop(0, CHIPS, exp_step, jnp.zeros((1, PAIR), F32))
    inverse = 1.0 / total

    gather_q[2].wave0()
    gather_q[0].wave1()
    for copy in cross_v:
        copy.wait_recv()

    att_t[...] = jnp.zeros_like(att_t)

    def value_step(s, carry):
        part = st[s] * inverse
        st[s] = part
        low = part.astype(BF)
        plow[s] = low
        att_t[...] += dot_tn(vb[s].reshape(PAIR, HD), low)
        return carry

    lax.fori_loop(0, CHIPS, value_step, 0)

    attended = att_t[...].T.astype(BF)
    for h in (0, 1):
        att[c, :, pl.ds(h * HD, HD)] = attended[h * TOK : (h + 1) * TOK]
    cross_a = remote(att.at[c], att.at[c], sib)
    cross_a.start()

    for copy in frag_x:
        copy.wait_recv()
    partial = fd[pl.ds(pl.multiple_of(x * 128, 128), 128), :]
    for d in range(3):
        partial = partial + fr[d].astype(F32)
    fs[...] = partial
    fz[...] = partial.astype(BF).reshape(4, 32, 128)
    frag_z = [remote(fz.at[lax.rem(zh + d, 4)], fzr.at[d - 1], z_peers[d - 1]) for d in (1, 2, 3)]
    for copy in frag_z:
        copy.start()

    gather_q[3].wave0()

    class Scatter:
        def __init__(self, p):
            self.p = p
            part = dw.at[p]
            a = self.a = GRAD_Z[p]
            b = PART - a
            a1, self.b1 = a // 2, a + b // 2
            self.a1 = a1
            far = tuple(enumerate((2, 6)))
            top, rest = pl.ds(0, a), pl.ds(a, b)
            self.to_z = remote(part.at[pl.ds(4, 4), rest], rz.at[p, :, pl.ds(0, b)], zp)
            self.a_up = [remote(part.at[s, pl.ds(0, a1)], ra1.at[p, i, pl.ds(0, a1)], yp) for i, s in far]
            self.a_down = [
                remote(part.at[s, pl.ds(a1, a - a1)], ra2.at[p, i, pl.ds(0, a - a1)], ym) for i, s in far
            ]
            self.b_up = remote(part.at[2, pl.ds(a, b // 2)], rb1.at[p, pl.ds(0, b // 2)], yp)
            self.b_down = remote(part.at[2, pl.ds(self.b1, b // 2)], rb2.at[p, pl.ds(0, b // 2)], ym)
            self.g = [
                remote(part.at[5, top], rg.at[p, 0, top], yp),
                remote(part.at[7, top], rg.at[p, 1, top], ym),
            ]
            self.fa = [
                remote(part.at[1, top], rf.at[p, 0, top], yp),
                remote(part.at[3, top], rf.at[p, 1, top], ym),
            ]
            self.fb = [
                remote(part.at[1, rest], rf.at[p, 0, rest], yp),
                remote(part.at[3, rest], rf.at[p, 1, rest], ym),
            ]
            self.last = remote(part.at[4, top], rw.at[p, top], zp)

        def add(self, s, lo, hi, *others):
            rows = pl.ds(lo, hi - lo)
            value = dw[self.p, s, rows, :].astype(F32)
            for other in others:
                value = value + other[...].astype(F32)
            dw[self.p, s, rows, :] = value.astype(BF)

        def begin(self):
            for copy in self.a_up + self.a_down:
                copy.start()
            self.to_z.start()

        def a_near(self):
            p, a, a1 = self.p, self.a, self.a1
            for copy in self.a_up:
                copy.wait_recv()
            self.add(5, 0, a1, ra1.at[p, 1, pl.ds(0, a1)])
            self.g[0].start()
            self.add(1, 0, a1, ra1.at[p, 0, pl.ds(0, a1)])
            self.fa[0].start()
            for copy in self.a_down:
                copy.wait_recv()
            self.add(7, a1, a, ra2.at[p, 1, pl.ds(0, a - a1)])
            self.g[1].start()
            self.add(3, a1, a, ra2.at[p, 0, pl.ds(0, a - a1)])
            self.fa[1].start()

        def a_last(self):
            p, a = self.p, self.a
            for copy in self.g:
                copy.wait_recv()
            self.add(4, 0, a, rg.at[p, 0, pl.ds(0, a)], rg.at[p, 1, pl.ds(0, a)])
            self.last.start()

        def b_far(self):
            p, a = self.p, self.a
            b = PART - a
            self.to_z.wait_recv()
            self.add(2, a, PART, rz.at[p, 2, pl.ds(0, b)])
            self.b_up.start()
            self.b_down.start()
            for s in (1, 3, 0):
                self.add(s, a, PART, rz.at[p, s, pl.ds(0, b)])

        def b_near(self):
            p, a, b1 = self.p, self.a, self.b1
            half = b1 - a
            self.b_up.wait_recv()
            self.add(1, a, b1, rb1.at[p, pl.ds(0, half)])
            self.fb[0].start()
            self.b_down.wait_recv()
            self.add(3, b1, PART, rb2.at[p, pl.ds(0, half)])
            self.fb[1].start()

        def end(self, first):
            p, a = self.p, self.a
            for copy in self.fa + self.fb + [self.last]:
                copy.wait_recv()
            value = dw[p, 0].astype(F32) + rf[p, 0].astype(F32) + rf[p, 1].astype(F32)
            top = value[:a] + rw[p, pl.ds(0, a), :].astype(F32)
            value = jnp.concatenate([top, value[a:]], axis=0)
            weight_out[0, :, pl.ds(first, PART)] = value.T.astype(BF)

    scatter_o, scatter_q, scatter_k = Scatter(0), Scatter(1), Scatter(2)

    def outer(p, left, right):
        def step(s, carry):
            dw[p, s] = dot(left, right[s].reshape(PAIR, BLK)).astype(BF)
            return carry

        lax.fori_loop(0, CHIPS, step, 0)

    for copy in load_g:
        copy.wait()
    for copy in cross_g:
        copy.wait_recv()
    gather_o[0].finish()
    gather_o[1].finish()
    agp[...] = jnp.zeros_like(agp)

    def grad_step(s, carry):
        part = dot(xg[s].reshape(PAIR, BLK), wg[s, :, pl.ds(QKV, QW)])
        agp[...] += part.reshape(2, TOK, QW)
        return carry

    lax.fori_loop(0, CHIPS, grad_step, 0)
    cross_p = remote(agp.at[o], agr, sib)
    cross_p.start()
    gather_q[2].wave1()
    gather_q[1].wave1()
    gather_q[0].wave2()
    cross_a.wait_recv()
    outer(0, att[...].reshape(PAIR, QW).T, xg)
    scatter_o.begin()
    cross_p.wait_recv()
    grad = (agp[c] + agr[...]).astype(BF)
    for h in (0, 1):
        gs[pl.ds(h * TOK, TOK), :] = grad[:, h * HD : (h + 1) * HD]
    row_delta = jnp.sum(att_t[...] * gs[...].astype(F32).T, axis=0, keepdims=True)

    dq_t[...] = jnp.zeros_like(dq_t)

    def cross_copy(s):
        return pltpu.make_async_remote_copy(
            src_ref=dkv.at[s, o],
            dst_ref=sk.at[s],
            send_sem=bsem.at[s],
            recv_sem=brsem.at[s],
            device_id=sib,
            device_id_type=MESH,
        )

    def back_step(s, carry):
        prob_grad = dot_nt(vb[s].reshape(PAIR, HD), gs[...])
        low = (st[s] * (prob_grad - row_delta) * scale).astype(BF)
        dq_t[...] += dot_tn(kb[s].reshape(PAIR, HD), low)
        dkv[s, :, :, pl.ds(0, HD)] = dot(low, qs[...]).astype(BF).reshape(2, TOK, HD)
        dkv[s, :, :, pl.ds(HD, HD)] = dot(plow[s], gs[...]).astype(BF).reshape(2, TOK, HD)
        cross_copy(s).start()
        return carry

    lax.fori_loop(0, CHIPS, back_step, 0)

    gather_q[3].wave1()
    gather_q[2].wave2()
    gather_q[1].wave2()

    def rotate(values_in):
        return values_in * cs[...] + pltpu.roll(values_in, HD // 2, 1) * sn[...]

    dq = dq_t[...].T
    for h in (0, 1):
        proj[c, :, pl.ds(h * HD, HD)] = rotate(dq[h * TOK : (h + 1) * TOK]).astype(BF)
    cross_q = remote(proj.at[c, :, pl.ds(0, QW)], proj.at[c, :, pl.ds(0, QW)], sib)
    cross_q.start()

    def pair_step(s, carry):
        cross_copy(s).wait_recv()
        ps[s] = (dkv[s, c].astype(F32) + sk[s].astype(F32)).astype(BF)
        return carry

    lax.fori_loop(0, CHIPS, pair_step, 0)
    send_d = [remote(ps.at[s], rk.at[back(s)], at(s // 4, s % 4)) for s in order]
    for copy in send_d:
        copy.start()

    scatter_o.a_near()
    for copy in load_x:
        copy.wait()
    for copy in cross_x:
        copy.wait_recv()
    cross_q.wait_recv()
    outer(1, proj[:, :, pl.ds(0, QW)].reshape(PAIR, QW).T, xi)
    scatter_q.begin()
    gather_q[3].wave2()
    scatter_o.b_far()

    for copy in frag_z:
        copy.wait_recv()
    home_z = pl.ds(pl.multiple_of(zh * 32, 32), 32)
    own = fs[home_z, :]
    for d in range(3):
        own = own + fzr[d].astype(F32)
    fs[home_z, :] = own
    frag_bz = [remote(fs.at[home_z], fs.at[home_z], dev) for dev in z_peers]
    for copy in frag_bz:
        copy.start()

    for copy in send_d:
        copy.wait_recv()

    def sum_step(s, carry):
        return carry + rk[s].astype(F32)

    kv = lax.fori_loop(1, CHIPS, sum_step, ps[0].astype(F32))
    proj[c, :, pl.ds(QW, HD)] = rotate(kv[:, :HD]).astype(BF)
    proj[c, :, pl.ds(QW + HD, HD)] = kv[:, HD:].astype(BF)
    cross_kv = remote(proj.at[c, :, pl.ds(QW, QW)], proj.at[c, :, pl.ds(QW, QW)], sib)
    cross_kv.start()
    cross_kv.wait_recv()
    outer(2, proj[:, :, pl.ds(QW, QW)].reshape(PAIR, QW).T, xi)
    scatter_k.begin()
    scatter_o.a_last()
    scatter_q.a_near()
    scatter_o.b_near()

    for copy in frag_bz:
        copy.wait_recv()
    home_x = pl.ds(pl.multiple_of(x * 128, 128), 128)
    for copy in frag_bz:
        copy.wait_send()
    fd[home_x, :] = fs[...]
    frag_bx = [remote(fs, fd.at[home_x], dev) for dev in x_peers]
    for copy in frag_bx:
        copy.start()

    scatter_k.a_near()
    scatter_q.b_far()

    for gather in gather_q:
        gather.finish()
    both = jnp.concatenate([proj[c], proj[o]], axis=0)
    cross_i = [remote(ig.at[s], input_out.at[0, :, columns(s, c)], sib) for s in range(CHIPS)]
    for s in range(CHIPS):
        block = dot_nt(both, wg[s, :, pl.ds(0, QKV)]).astype(BF)
        input_out[0, :, columns(s, c)] = block[:TOK]
        ig[s] = block[TOK:]
        cross_i[s].start()

    scatter_q.a_last()
    scatter_k.b_far()
    scatter_k.a_last()
    scatter_q.b_near()
    scatter_k.b_near()

    for copy in frag_bx:
        copy.wait_recv()
    for copy in load_t:
        copy.wait()
    outer_grad = fd[...] / replicas
    moment_next = outer_beta * fm[...] + outer_grad
    moment_out[...] = moment_next
    params_out[...] = fp[...] - outer_rate * (outer_grad + outer_beta * moment_next)

    scatter_o.end(QKV)
    scatter_q.end(0)
    scatter_k.end(QW)

    for copy in cross_i:
        copy.wait_recv()
    for copy in made:
        if not any(copy is other for other in frag_bz):
            copy.wait_send()

    def drain(s, carry):
        cross_copy(s).wait_send()
        return carry

    lax.fori_loop(0, CHIPS, drain, 0)


def body(inputs, out_grad, queries, key_states, value_states, weights, frag_delta, frag_params, frag_moment):
    anywhere = pl.BlockSpec(memory_space=pl.ANY)
    vm = pltpu.VMEM
    dma = pltpu.SemaphoreType.DMA
    return pl.pallas_call(
        functools.partial(kernel, float(lax.axis_size("replica"))),
        out_shape=(
            vm(inputs.shape, BF),
            vm(weights.shape, BF),
            vm(frag_params.shape, F32),
            vm(frag_moment.shape, F32),
        ),
        in_specs=[anywhere] * 9,
        out_specs=(pl.BlockSpec(memory_space=pltpu.VMEM),) * 4,
        scratch_shapes=[
            vm((CHIPS, 2, TOK, BLK), BF),
            vm((CHIPS, 2, TOK, BLK), BF),
            vm((CHIPS, BLK, WC), BF),
            vm((CHIPS, 2, TOK, HD), BF),
            vm((CHIPS, 2, TOK, HD), BF),
            vm((PAIR, HD), BF),
            vm((CHIPS, PAIR, PAIR), F32),
            vm((CHIPS, PAIR, PAIR), BF),
                vm((HD, PAIR), F32),
            vm((HD, PAIR), F32),
            vm((PAIR, HD), BF),
            vm((2, TOK, QW), F32),
            vm((TOK, QW), F32),
            vm((2, TOK, QW), BF),
            vm((2, TOK, QKV), BF),
            vm((CHIPS, 2, TOK, QW), BF),
            vm((CHIPS, TOK, QW), BF),
            vm((CHIPS, TOK, QW), BF),
            vm((CHIPS, TOK, QW), BF),
            vm((3, CHIPS, PART, BLK), BF),
            vm((3, YS, MOST_B, BLK), BF),
            vm((3, 2, MOST_A // 2, BLK), BF),
            vm((3, 2, MOST_A // 2, BLK), BF),
            vm((3, MOST_B // 2, BLK), BF),
            vm((3, MOST_B // 2, BLK), BF),
            vm((3, 2, PART, BLK), BF),
            vm((3, 2, MOST_A, BLK), BF),
            vm((3, MOST_A, BLK), BF),
            vm((CHIPS, TOK, BLK), BF),
            vm((TOK, HD), F32),
            vm((TOK, HD), F32),
            vm((512, 128), F32),
            vm((4, 128, 128), BF),
            vm((3, 128, 128), BF),
            vm((4, 32, 128), BF),
            vm((3, 32, 128), BF),
            vm((128, 128), F32),
            vm((512, 128), F32),
            vm((512, 128), F32),
            dma((64,)),
            dma((256,)),
            dma((256,)),
            dma((CHIPS,)),
            dma((CHIPS,)),
        ],
        compiler_params=pltpu.CompilerParams(
            collective_id=0, has_side_effects=True, vmem_limit_bytes=50 * 2**20
        ),
    )(inputs, out_grad, queries, key_states, value_states, weights, frag_delta, frag_params, frag_moment)


def solution(mesh):
    rows = P("replica", "fsdp", None)
    shared = P("fsdp", None)
    return jax.shard_map(
        body,
        mesh=mesh,
        in_specs=(rows,) * 7 + (shared,) * 2,
        out_specs=(rows, rows, shared, shared),
        check_vma=False,
    )
```

```python
import functools
import math

import jax
import jax.numpy as jnp
from jax import lax
from jax.experimental import pallas as pl
from jax.experimental.pallas import tpu as pltpu
from jax.sharding import PartitionSpec as P

rope_base = 500000.0
outer_rate = 0.7
outer_beta = 0.9
masked_score = -1e30

BF = jnp.bfloat16
F32 = jnp.float32
MESH = pl.DeviceIdType.MESH

TOK = 192
PAIR = 2 * TOK
HD = 128
QW = 256
BLK = 512
WC = 768
QKV = 512
CHIPS = 8
YS = 4

WEIGHT_Z = 288
KEY_Z = 112
PARTS = (
    (192, 256, 112, 48, 48),
    (256, 512, 160, 80, 48),
    (256, 512, 128, 64, 64),
    (128, 512, 80, 48, 16),
    (128, 512, 80, 48, 16),
)
PART = 256
SEMS = 132

ORDER = (
    "K.w0", "V.w0", "o0.w0", "g.x", "f.x", "loads", "K.w1", "V.w1", "o1.w0", "V.w2", "K.w2",
    "o0.w1", "o1.w1", "kx", "vx", "q0.w0", "score", "o0.w2", "o1.w2", "q1.w0", "q2.w0", "value",
    "f.z", "q3.w0", "grad", "so.S", "q0.w1", "back", "q3.w1", "dq", "pair", "q1.w1", "so.b2", "d.S",
    "so.a3", "sq.S", "f.bz", "d.b2", "d.a3", "q1.w2", "so.b3", "d.b3", "d.a4", "q2.w1", "sq.a3",
    "kv", "q3.w2", "sk0.S", "q0.w2", "q2.w2", "sk1.S", "so.a4", "sk0.a3", "sq.b2", "f.bx", "sq.a4",
    "sk1.a3", "sk0.b2", "ig", "f.end", "sk1.b2", "sq.b3", "sk1.a4", "sk0.a4", "sk1.b3", "sk0.b3",
    "sq.fin", "so.fin", "sk1.fin", "sk0.fin",
)

NT = (((1,), (1,)), ((), ()))
TN = (((0,), (0,)), ((), ()))


def dot(a, b):
    return jnp.dot(a, b, preferred_element_type=F32)


def dot_nt(a, b):
    return lax.dot_general(a, b, NT, preferred_element_type=F32)


def dot_tn(a, b):
    return lax.dot_general(a, b, TN, preferred_element_type=F32)


def kernel(
    replicas,
    inputs,
    out_grad,
    queries,
    keys,
    values,
    weights,
    delta,
    params,
    moment,
    input_out,
    weight_out,
    params_out,
    moment_out,
    xi,
    xg,
    wg,
    kb,
    vb,
    qs,
    st,
    plow,
    att_t,
    dq_t,
    gs,
    agp,
    agr,
    att,
    proj,
    dkv,
    sk,
    ig,
    cs,
    sn,
    fd,
    fb,
    fr,
    fz,
    fzr,
    fs,
    fp,
    fm,
    sems,
    *parts,
):
    r = lax.axis_index("replica")
    f = lax.axis_index("fsdp")
    c = lax.rem(f, 2)
    y = lax.rem(f // 2, YS)
    z = f // (2 * YS)
    o = 1 - c
    x = lax.rem(r, 4)
    zh = r // 4

    def chip(dz, dy):
        return lax.rem(z + dz, 2) * YS + lax.rem(y + dy, YS)

    def at(dz, dy, core=None):
        return (r, chip(dz, dy) * 2 + (c if core is None else core))

    yp, ym, zp, sib = at(0, 1), at(0, 3), at(1, 0), at(0, 0, o)

    def back(s):
        return (s // 4) * 4 + (4 - s % 4) % 4

    taken = []

    def sem():
        taken.append(1)
        return sems.at[len(taken) - 1]

    def remote(src, dst, dev, sent, landed):
        return pltpu.make_async_remote_copy(
            src_ref=src,
            dst_ref=dst,
            send_sem=sent,
            recv_sem=landed,
            device_id=dev,
            device_id_type=MESH,
        )

    class Load:
        def __init__(self, whole, pairs):
            self.whole, self.sem = whole, sem()
            for src, dst in pairs:
                pltpu.make_async_copy(src, dst, self.sem).start()

        def wait(self):
            pltpu.make_async_copy(self.whole, self.whole, self.sem).wait()

    class Cross:
        def __init__(self, whole, triples):
            self.sent, self.landed = sem(), sem()
            self.all = remote(whole, whole, sib, self.sent, self.landed)
            self.copies = [remote(src, dst, dev, self.sent, self.landed) for src, dst, dev in triples]

        def start(self):
            for copy in self.copies:
                copy.start()

        def wait_recv(self):
            self.all.wait_recv()

        def wait_send(self):
            self.all.wait_send()

    def slot_chip(s):
        return lax.rem(z + s // 4, 2) * YS + lax.rem(y + s % 4, YS)

    def columns(s, core):
        return pl.ds(pl.multiple_of((slot_chip(s) * 2 + core) * BLK, BLK), BLK)

    load_q = Load(qs, [(queries.at[0, :, pl.ds(h * HD, HD)], qs.at[pl.ds(h * TOK, TOK)]) for h in (0, 1)])
    load_k = Load(kb.at[0, c], [(keys.at[0], kb.at[0, c])])
    load_v = Load(vb.at[0, c], [(values.at[0], vb.at[0, c])])
    load_w = Load(wg.at[0], [(weights.at[0], wg.at[0])])
    load_d = Load(fd, [(delta.at[0], fd)])
    load_g = Load(xg.at[:, c], [(out_grad.at[0, :, columns(s, c)], xg.at[s, c]) for s in range(CHIPS)])
    load_x = Load(xi.at[:, c], [(inputs.at[0, :, columns(s, c)], xi.at[s, c]) for s in range(CHIPS)])
    load_p = Load(fp, [(params, fp)])
    load_m = Load(fm, [(moment, fm)])

    peers = [yp, ym, zp, sib]
    x_peers = [(zh * 4 + lax.rem(x + d, 4), f) for d in (1, 2, 3)]
    z_peers = [(lax.rem(zh + d, 4) * 4 + x, f) for d in (1, 2, 3)]
    barrier = pltpu.get_barrier_semaphore()
    for dev in peers + x_peers + z_peers:
        pl.semaphore_signal(barrier, inc=1, device_id=dev, device_id_type=MESH)
    pos = (f * TOK + lax.broadcasted_iota(jnp.int32, (TOK, HD), 0)).astype(F32)
    lane = lax.broadcasted_iota(jnp.int32, (1, HD), 1)
    step_of = jnp.where(lane >= HD // 2, lane - HD // 2, lane).astype(F32)
    angles = pos * jnp.exp(-math.log(rope_base) * 2.0 * step_of / HD)
    cs[...] = jnp.cos(angles)
    sine = jnp.sin(angles)
    sn[...] = jnp.where(lane >= HD // 2, -sine, sine)
    pl.semaphore_wait(barrier, len(peers) + 6)

    class Gather:
        def __init__(self, own, rows, extent, first, sent, rest, two, near):
            def move(src, dst, lo, hi, dev, landed):
                return remote(rows(src, lo, hi), rows(dst, lo, hi), dev, sent, landed)

            half = first // 32 * 16
            self.s3 = remote(own, rows(3, 0, extent), yp, sent, sem())
            self.s1 = remote(own, rows(1, 0, extent), ym, sent, sem())
            self.s4 = remote(own, rows(4, 0, extent), zp, sent, sem())
            far, close = sem(), sem()
            self.s2a = move(1, 2, 0, extent // 2, ym, far)
            self.s2b = move(3, 2, extent // 2, extent, yp, far)
            self.s7a = move(4, 7, 0, first, yp, close)
            self.s5a = move(4, 5, 0, first, ym, close)
            self.s5b = move(1, 5, first, extent, zp, rest)
            self.s7b = move(3, 7, first, extent, zp, rest)
            self.s6b = move(2, 6, first, extent, zp, rest)
            self.s6a1 = move(5, 6, 0, half, ym, rest)
            self.s6a2 = move(7, 6, half, first, yp, rest)
            self.two = remote(two, two, sib, sent, far)
            self.near = remote(near, near, sib, sent, close)

        def wave0(self):
            self.s3.start()
            self.s1.start()
            self.s4.start()

        def wave1(self):
            self.s1.wait_recv()
            self.s2a.start()
            self.s5b.start()
            self.s3.wait_recv()
            self.s2b.start()
            self.s7b.start()
            self.s4.wait_recv()
            self.s7a.start()
            self.s5a.start()

        def wave2(self):
            self.two.wait_recv()
            self.s6b.start()
            self.near.wait_recv()
            self.s6a1.start()
            self.s6a2.start()

    def gather_states(source, target):
        sent, rest = sem(), sem()
        gather = Gather(
            source.at[0],
            lambda s, lo, hi: target.at[s, c, pl.ds(lo, hi - lo)],
            TOK,
            KEY_Z,
            sent,
            rest,
            target.at[0, c],
            qs.at[pl.ds(0, 2 * KEY_Z)],
        )
        left = qs.at[pl.ds(0, 3 * (TOK - KEY_Z) + KEY_Z)]
        every = target.at[pl.ds(0, CHIPS - 1), c]
        return gather, remote(every, left, sib, sent, rest)

    sent_w, rest_o, rest_q = sem(), sem(), sem()

    def gather_weights(first, rest):
        cols = pl.ds(first, HD)
        return Gather(
            weights.at[0, :, cols],
            lambda s, lo, hi: wg.at[s, pl.ds(lo, hi - lo), cols],
            BLK,
            WEIGHT_Z,
            sent_w,
            rest,
            wg.at[0, :, cols],
            wg.at[0, pl.ds(0, 2 * WEIGHT_Z * HD // WC), :],
        )

    def left_of(pieces):
        rows = pieces * (3 * (BLK - WEIGHT_Z) + WEIGHT_Z) * HD // WC // 5
        return wg.at[pl.ds(0, 5), pl.ds(0, rows), :]

    gather_key, all_key = gather_states(keys, kb)
    gather_value, all_value = gather_states(values, vb)
    gather_o = [gather_weights(QKV + HD * i, rest_o) for i in range(2)]
    gather_q = [gather_weights(HD * i, rest_q) for i in range(4)]
    all_o = remote(wg.at[pl.ds(0, CHIPS - 1)], left_of(2), sib, sent_w, rest_o)
    all_q = remote(wg.at[pl.ds(0, CHIPS - 1)], left_of(4), sib, sent_w, rest_q)
    cross_k = Cross(
        kb.at[:, c], [(keys.at[0] if s == 0 else kb.at[s, c], kb.at[s, c], sib) for s in range(CHIPS)]
    )
    cross_v = Cross(
        vb.at[:, c], [(values.at[0] if s == 0 else vb.at[s, c], vb.at[s, c], sib) for s in range(CHIPS)]
    )

    cross_g = Cross(
        xg.at[:, c], [(out_grad.at[0, :, columns(s, o)], xg.at[s, c], sib) for s in range(CHIPS)]
    )
    cross_x = Cross(
        xi.at[:, c], [(inputs.at[0, :, columns(s, o)], xi.at[s, c], sib) for s in range(CHIPS)]
    )
    half_q, half_kv = proj.at[c, :, pl.ds(0, QW)], proj.at[c, :, pl.ds(QW, QW)]
    cross_a = Cross(att.at[c], [(att.at[c], att.at[c], sib)])
    cross_p = Cross(agr, [(agp.at[o], agr, sib)])
    cross_q = Cross(half_q, [(half_q, half_q, sib)])
    cross_kv = Cross(half_kv, [(half_kv, half_kv, sib)])
    cross_i = Cross(ig, [(ig.at[s], input_out.at[0, :, columns(s, c)], sib) for s in range(CHIPS)])
    sent_d, landed_d = sem(), sem()
    cross_d = remote(sk, sk, sib, sent_d, landed_d)

    home_x = pl.ds(pl.multiple_of(x * 128, 128), 128)
    home_z = pl.ds(pl.multiple_of(zh * 32, 32), 32)
    frag_x = Cross(fr, [(fb.at[lax.rem(x + d, 4)], fr.at[d - 1], x_peers[d - 1]) for d in (1, 2, 3)])
    frag_z = Cross(fzr, [(fz.at[lax.rem(zh + d, 4)], fzr.at[d - 1], z_peers[d - 1]) for d in (1, 2, 3)])
    frag_bz = Cross(fs.at[pl.ds(0, 96)], [(fs.at[home_z], fs.at[home_z], dev) for dev in z_peers])
    frag_bx = Cross(fd.at[pl.ds(0, 384)], [(fs, fd.at[home_x], dev) for dev in x_peers])

    def fragment_start():
        load_d.wait()
        for j in range(4):
            fb[j] = fd[pl.ds(j * 128, 128), :].astype(BF)
        frag_x.start()

    def fragment_over_z():
        frag_x.wait_recv()
        partial = fd[home_x, :]
        for d in range(3):
            partial = partial + fr[d].astype(F32)
        fs[...] = partial
        fz[...] = partial.astype(BF).reshape(4, 32, 128)
        frag_z.start()

    def fragment_back_z():
        frag_z.wait_recv()
        own = fs[home_z, :]
        for d in range(3):
            own = own + fzr[d].astype(F32)
        fs[home_z, :] = own
        frag_bz.start()

    def fragment_back_x():
        frag_bz.wait_recv()
        frag_bz.wait_send()
        fd[home_x, :] = fs[...]
        frag_bx.start()

    def fragment_end():
        frag_bx.wait_recv()
        load_p.wait()
        load_m.wait()
        outer_grad = fd[...] / replicas
        moment_next = outer_beta * fm[...] + outer_grad
        moment_out[...] = moment_next
        params_out[...] = fp[...] - outer_rate * (outer_grad + outer_beta * moment_next)

    held = {}
    scale = 1.0 / math.sqrt(HD)

    class Scatter:
        def __init__(self, n):
            part, rzp, up, down, bup, bdown, near, cross, final = parts[9 * n : 9 * n + 9]
            extent, _, a, a1, half = PARTS[n]
            self.part, self.a, self.a1, self.b1, self.extent = part, a, a1, a + half, extent
            self.rz, self.up, self.down, self.bup, self.bdown = rzp, up, down, bup, bdown
            self.near, self.cross, self.final = near, cross, final
            far = tuple(enumerate((2, 6)))
            top, rest = pl.ds(0, a), pl.ds(a, extent - a)
            sent = sem()
            self.sent = remote(part.at[pl.ds(0, CHIPS - 1)], part.at[0], sib, sent, sent)
            self.to_z = remote(part.at[pl.ds(4, 4), rest], rzp, zp, sent, sem())
            landed = sem()
            self.a_up = [remote(part.at[s, pl.ds(0, a1)], up.at[i], yp, sent, landed) for i, s in far]
            self.up_all = remote(up, up, sib, sent, landed)
            landed = sem()
            self.a_down = [
                remote(part.at[s, pl.ds(a1, a - a1)], down.at[i], ym, sent, landed) for i, s in far
            ]
            self.down_all = remote(down, down, sib, sent, landed)
            self.b_up = remote(part.at[2, pl.ds(a, half)], bup, yp, sent, sem())
            self.b_down = remote(part.at[2, pl.ds(a + half, extent - a - half)], bdown, ym, sent, sem())
            landed = sem()
            self.g = [
                remote(part.at[5, top], cross.at[0], yp, sent, landed),
                remote(part.at[7, top], cross.at[1], ym, sent, landed),
            ]
            self.g_all = remote(cross, cross, sib, sent, landed)
            landed = sem()
            self.fa = [
                remote(part.at[1, top], near.at[0, top], yp, sent, landed),
                remote(part.at[3, top], near.at[1, top], ym, sent, landed),
            ]
            self.fb = [
                remote(part.at[1, rest], near.at[0, rest], yp, sent, landed),
                remote(part.at[3, rest], near.at[1, rest], ym, sent, landed),
            ]
            self.f_all = remote(near, near, sib, sent, landed)
            self.last = remote(part.at[4, top], final, zp, sent, sem())

        def add(self, s, lo, hi, *others):
            rows = pl.ds(lo, hi - lo)
            value = self.part[s, rows, :].astype(F32)
            for other in others:
                value = value + other[...].astype(F32)
            self.part[s, rows, :] = value.astype(BF)

        def begin(self):
            for copy in self.a_up + self.a_down:
                copy.start()
            self.to_z.start()

        def a_near(self):
            a, a1 = self.a, self.a1
            self.up_all.wait_recv()
            self.add(5, 0, a1, self.up.at[1])
            self.g[0].start()
            self.add(1, 0, a1, self.up.at[0])
            self.fa[0].start()
            self.down_all.wait_recv()
            self.add(7, a1, a, self.down.at[1])
            self.g[1].start()
            self.add(3, a1, a, self.down.at[0])
            self.fa[1].start()

        def a_last(self):
            self.g_all.wait_recv()
            self.add(4, 0, self.a, self.cross.at[0], self.cross.at[1])
            self.last.start()

        def b_far(self):
            a, extent = self.a, self.extent
            self.to_z.wait_recv()
            self.add(2, a, extent, self.rz.at[2])
            self.b_up.start()
            self.b_down.start()
            for s in (1, 3, 0):
                self.add(s, a, extent, self.rz.at[s])

        def b_near(self):
            a, b1 = self.a, self.b1
            self.b_up.wait_recv()
            self.add(1, a, b1, self.bup)
            self.fb[0].start()
            self.b_down.wait_recv()
            self.add(3, b1, self.extent, self.bdown)
            self.fb[1].start()

        def total(self):
            a = self.a
            self.f_all.wait_recv()
            self.last.wait_recv()
            value = self.part[0].astype(F32) + self.near[0].astype(F32) + self.near[1].astype(F32)
            top = value[:a] + self.final[...].astype(F32)
            return jnp.concatenate([top, value[a:]], axis=0)

    def finish_part(scatter, first):
        weight_out[0, :, pl.ds(first, scatter.extent)] = scatter.total().T.astype(BF)

    scatter_d, scatter_o, scatter_q, scatter_k, scatter_v = [Scatter(n) for n in range(5)]

    def outer(scatter, left, right):
        def step(s, carry):
            scatter.part[s] = dot(left, right[s].reshape(PAIR, BLK)).astype(BF)
            return carry

        lax.fori_loop(0, CHIPS, step, 0)

    def first_loads():
        load_k.wait()
        load_v.wait()
        load_w.wait()

    def cross_keys():
        all_key.wait_recv()
        cross_k.start()

    def cross_values():
        all_value.wait_recv()
        cross_v.start()
        cross_x.start()

    def score_step(s, peak):
        part = dot_nt(kb[s].reshape(PAIR, HD), qs[...]) * scale
        key_pos = slot_chip(s) * PAIR + lax.broadcasted_iota(jnp.int32, (PAIR, PAIR), 0)
        lane = lax.broadcasted_iota(jnp.int32, (1, PAIR), 1)
        query_pos = f * TOK + jnp.where(lane >= TOK, lane - TOK, lane)
        part = jnp.where(key_pos <= query_pos, part, masked_score)
        st[s] = part
        return jnp.maximum(peak, jnp.max(part, axis=0, keepdims=True))

    def score():
        load_q.wait()
        cross_k.wait_recv()
        peak = lax.fori_loop(0, CHIPS, score_step, jnp.full((1, PAIR), masked_score, F32))

        def exp_step(s, total):
            part = jnp.exp(st[s] - peak)
            st[s] = part
            return total + jnp.sum(part, axis=0, keepdims=True)

        total = lax.fori_loop(0, CHIPS, exp_step, jnp.zeros((1, PAIR), F32))
        held["inverse"] = 1.0 / total

    def value():
        cross_v.wait_recv()
        att_t[...] = jnp.zeros_like(att_t)
        inverse = held["inverse"]

        def value_step(s, carry):
            part = st[s] * inverse
            st[s] = part
            low = part.astype(BF)
            plow[s] = low
            att_t[...] += dot_tn(vb[s].reshape(PAIR, HD), low)
            return carry

        lax.fori_loop(0, CHIPS, value_step, 0)
        attended = att_t[...].T.astype(BF)
        for h in (0, 1):
            att[c, :, pl.ds(h * HD, HD)] = attended[h * TOK : (h + 1) * TOK]
        cross_a.start()

    def grad():
        load_g.wait()
        cross_g.wait_recv()
        all_o.wait_recv()
        agp[...] = jnp.zeros_like(agp)

        def grad_step(s, carry):
            part = dot(xg[s].reshape(PAIR, BLK), wg[s, :, pl.ds(QKV, QW)])
            agp[...] += part.reshape(2, TOK, QW)
            return carry

        lax.fori_loop(0, CHIPS, grad_step, 0)
        cross_p.start()

    def back_all():
        cross_p.wait_recv()
        own = (agp[c] + agr[...]).astype(BF)
        for h in (0, 1):
            gs[pl.ds(h * TOK, TOK), :] = own[:, h * HD : (h + 1) * HD]
        row_delta = jnp.sum(att_t[...] * gs[...].astype(F32).T, axis=0, keepdims=True)
        dq_t[...] = jnp.zeros_like(dq_t)

        def back_step(s, carry):
            prob_grad = dot_nt(vb[s].reshape(PAIR, HD), gs[...])
            low = (st[s] * (prob_grad - row_delta) * scale).astype(BF)
            dq_t[...] += dot_tn(kb[s].reshape(PAIR, HD), low)
            dkv[s, :, :, pl.ds(0, HD)] = dot(low, qs[...]).astype(BF).reshape(2, TOK, HD)
            dkv[s, :, :, pl.ds(HD, HD)] = dot(plow[s], gs[...]).astype(BF).reshape(2, TOK, HD)
            remote(dkv.at[s, o], sk.at[s], sib, sent_d, landed_d).start()
            return carry

        lax.fori_loop(0, CHIPS, back_step, 0)

    def rotate(values_in):
        return values_in * cs[...] + pltpu.roll(values_in, HD // 2, 1) * sn[...]

    def query_grad():
        dq = dq_t[...].T
        for h in (0, 1):
            proj[c, :, pl.ds(h * HD, HD)] = rotate(dq[h * TOK : (h + 1) * TOK]).astype(BF)
        cross_q.start()

    def pair():
        cross_d.wait_recv()

        def pair_step(s, carry):
            scatter_d.part[s] = (dkv[s, c].astype(F32) + sk[s].astype(F32)).astype(BF)
            return carry

        lax.fori_loop(0, CHIPS, pair_step, 0)

    def key_value_grad():
        kv = scatter_d.total()
        proj[c, :, pl.ds(QW, HD)] = rotate(kv[:, :HD]).astype(BF)
        proj[c, :, pl.ds(QW + HD, HD)] = kv[:, HD:].astype(BF)
        cross_kv.start()

    def out_begin():
        cross_a.wait_recv()
        outer(scatter_o, att[...].reshape(PAIR, QW).T, xg)
        scatter_o.begin()

    def query_begin():
        load_x.wait()
        cross_x.wait_recv()
        cross_q.wait_recv()
        outer(scatter_q, proj[:, :, pl.ds(0, QW)].reshape(PAIR, QW).T, xi)
        scatter_q.begin()

    def key_begin():
        cross_kv.wait_recv()
        outer(scatter_k, proj[:, :, pl.ds(QW, HD)].reshape(PAIR, HD).T, xi)
        scatter_k.begin()

    def value_begin():
        outer(scatter_v, proj[:, :, pl.ds(QW + HD, HD)].reshape(PAIR, HD).T, xi)
        scatter_v.begin()

    def inputs_grad():
        all_q.wait_recv()
        both = jnp.concatenate([proj[c], proj[o]], axis=0)
        for s in range(CHIPS):
            block = dot_nt(both, wg[s, :, pl.ds(0, QKV)]).astype(BF)
            input_out[0, :, columns(s, c)] = block[:TOK]
            ig[s] = block[TOK:]
            cross_i.copies[s].start()

    tasks = {
        "loads": first_loads,
        "g.x": cross_g.start,
        "kx": cross_keys,
        "vx": cross_values,
        "score": score,
        "value": value,
        "grad": grad,
        "back": back_all,
        "dq": query_grad,
        "pair": pair,
        "kv": key_value_grad,
        "ig": inputs_grad,
        "f.x": fragment_start,
        "f.z": fragment_over_z,
        "f.bz": fragment_back_z,
        "f.bx": fragment_back_x,
        "f.end": fragment_end,
        "so.S": out_begin,
        "sq.S": query_begin,
        "sk0.S": key_begin,
        "sk1.S": value_begin,
        "d.S": scatter_d.begin,
    }
    gathers = {"K": gather_key, "V": gather_value}
    gathers.update({"o%d" % i: gather for i, gather in enumerate(gather_o)})
    gathers.update({"q%d" % i: gather for i, gather in enumerate(gather_q)})
    for name, gather in gathers.items():
        tasks.update({name + ".w0": gather.wave0, name + ".w1": gather.wave1, name + ".w2": gather.wave2})
    ends = (("d", scatter_d, None), ("so", scatter_o, QKV), ("sq", scatter_q, 0))
    for name, scatter, first in ends + (("sk0", scatter_k, QW), ("sk1", scatter_v, QW + HD)):
        tasks.update({name + ".a3": scatter.a_near, name + ".a4": scatter.a_last})
        tasks.update({name + ".b2": scatter.b_far, name + ".b3": scatter.b_near})
        tasks[name + ".fin"] = functools.partial(finish_part, scatter, first)
    for name in ORDER:
        tasks[name]()

    cross_i.wait_recv()
    for group in (cross_k, cross_v, cross_g, cross_x, cross_a, cross_p, cross_q, cross_kv, cross_i):
        group.wait_send()
    for group in (frag_x, frag_z, frag_bx, all_key, all_value, all_o, cross_d):
        group.wait_send()
    for scatter in (scatter_o, scatter_q, scatter_k, scatter_v, scatter_d):
        scatter.sent.wait_send()
    assert len(taken) <= SEMS


def part_buffers(rows, cols, a, a1, half):
    b = rows - a
    shapes = (
        (CHIPS, rows, cols),
        (YS, b, cols),
        (2, a1, cols),
        (2, a - a1, cols),
        (half, cols),
        (b - half, cols),
        (2, rows, cols),
        (2, a, cols),
        (a, cols),
    )
    return [pltpu.VMEM(shape, BF) for shape in shapes]


def store(*refs):
    sems = refs[8]
    copies = [pltpu.make_async_copy(refs[i], refs[4 + i], sems.at[i]) for i in range(4)]
    for copy in copies:
        copy.start()
    for copy in copies:
        copy.wait()


def body(inputs, out_grad, queries, key_states, value_states, weights, frag_delta, frag_params, frag_moment):
    anywhere = pl.BlockSpec(memory_space=pl.ANY)
    vm = pltpu.VMEM
    dma = pltpu.SemaphoreType.DMA
    results = pl.pallas_call(
        functools.partial(kernel, float(lax.axis_size("replica"))),
        out_shape=(
            vm(inputs.shape, BF),
            vm(weights.shape, BF),
            vm(frag_params.shape, F32),
            vm(frag_moment.shape, F32),
        ),
        in_specs=[anywhere] * 9,
        out_specs=(pl.BlockSpec(memory_space=pltpu.VMEM),) * 4,
        scratch_shapes=[
            vm((CHIPS, 2, TOK, BLK), BF),
            vm((CHIPS, 2, TOK, BLK), BF),
            vm((CHIPS, BLK, WC), BF),
            vm((CHIPS, 2, TOK, HD), BF),
            vm((CHIPS, 2, TOK, HD), BF),
            vm((PAIR, HD), BF),
            vm((CHIPS, PAIR, PAIR), F32),
            vm((CHIPS, PAIR, PAIR), BF),
                vm((HD, PAIR), F32),
            vm((HD, PAIR), F32),
            vm((PAIR, HD), BF),
            vm((2, TOK, QW), F32),
            vm((TOK, QW), F32),
            vm((2, TOK, QW), BF),
            vm((2, TOK, QKV), BF),
            vm((CHIPS, 2, TOK, QW), BF),
            vm((CHIPS, TOK, QW), BF),
            vm((CHIPS, TOK, BLK), BF),
            vm((TOK, HD), F32),
            vm((TOK, HD), F32),
            vm((512, 128), F32),
            vm((4, 128, 128), BF),
            vm((3, 128, 128), BF),
            vm((4, 32, 128), BF),
            vm((3, 32, 128), BF),
            vm((128, 128), F32),
            vm((512, 128), F32),
            vm((512, 128), F32),
            dma((SEMS,)),
        ]
        + [shape for part in PARTS for shape in part_buffers(*part)],
        compiler_params=pltpu.CompilerParams(
            collective_id=0, has_side_effects=True, vmem_limit_bytes=58 * 2**20
        ),
    )(inputs, out_grad, queries, key_states, value_states, weights, frag_delta, frag_params, frag_moment)
    return pl.pallas_call(
        store,
        out_shape=[jax.ShapeDtypeStruct(value.shape, value.dtype) for value in results],
        in_specs=[pl.BlockSpec(memory_space=pl.ANY)] * 4,
        out_specs=[pl.BlockSpec(memory_space=pl.ANY)] * 4,
        scratch_shapes=[dma((4,))],
        compiler_params=pltpu.CompilerParams(vmem_limit_bytes=2**20),
    )(*[pltpu.with_memory_space_constraint(value, pltpu.VMEM) for value in results])


def solution(mesh):
    rows = P("replica", "fsdp", None)
    shared = P("fsdp", None)
    return jax.shard_map(
        body,
        mesh=mesh,
        in_specs=(rows,) * 7 + (shared,) * 2,
        out_specs=(rows, rows, shared, shared),
        check_vma=False,
    )
```
